32 devices in a mesh: groups: 2 (over y), tp: 16 (over z, x, core).
Axes of the slice: x: 2, y: 2, z: 4, core: 2. Of those that a mesh axis runs over, the one named last changes fastest.
Arguments:
- hidden: bfloat16 [64, 26624], P('groups', 'tp'), parts along dimension 0, may hold values from -6 to 6
- down_weight: bfloat16 [26624, 16384], P('tp'), may hold values from -0.0546875 to 0.0546875
- residual: bfloat16 [64, 16384], P('groups', 'tp'), parts along dimension 0, may hold values from -6 to 6
Outputs:
- out_values: bfloat16 [64, 16384], P('groups'), parts along dimension 0
- out_scales: bfloat16 [64, 128], P('groups'), parts along dimension 0
The draws below stay inside these ranges and needn't reach their ends.
There are 2 independent parts, one for each index of `groups`. The reference program is written for one: setup_inputs(seed, part) draws one part's arguments, and reference() takes and returns one part's arrays. A program takes and returns all parts, laid end to end along the dimension named above; an argument that names none is the same for every part. Nothing has to cross between parts.
All inputs are finite; a program needn't handle non-finite values. Where the reference program divides by a largest or mean magnitude, that divisor is 1e-20 or more.
Results may differ from the reference program's by a relative error of at most 0.0095.
Values may be sent and summed in bfloat16 or wider, within the bound.
A program may use at most 128 MiB of HBM per device.

```python
import jax
import jax.numpy as jnp
from jax import lax

D = 16384
FF = 26624
BLOCK = 128
ROWS = 32
N_TP = 16


def spiked(entries, rng, source, target, blocks, factor):
    def block_of(position):
        return (jnp.arange(entries.shape[position]) // (entries.shape[position] // blocks)).reshape((-1,) + (1,) * (entries.ndim - 1 - position))

    first = jax.random.permutation(rng, blocks)[block_of(target)]
    second = (block_of(target) + blocks // 2) % blocks
    return jnp.where((block_of(source) == first) | (block_of(source) == second), factor * entries, entries)


def block_scale(rng, extent, pieces, smallest, high):
    level = 1.0
    for dim, parts in pieces:
        heights = jax.random.uniform(jax.random.fold_in(jax.random.fold_in(rng, 6), dim), (parts,), jnp.float32, smallest / len(pieces), high / len(pieces))
        level = level * jnp.repeat(jnp.exp(heights), extent[dim] // parts).reshape((-1,) + (1,) * (len(extent) - 1 - dim))
    return level


def scatter_about(own_key, extent, scale, bound, split=(), kind=jnp.bfloat16):
    result = jax.random.normal(own_key, extent, jnp.float32) * scale
    if len(split) > 0:
        result = block_scale(own_key, extent, split, -0.22, 0.18) * result
    return jnp.clip(result, min=-bound, max=bound).astype(kind)


def heavy_noise(own_key, shape, scale, reach, split, heavy, kind=jnp.bfloat16):
    result = scale * jax.random.normal(own_key, shape, jnp.float32)
    if split:
        result = result * block_scale(own_key, shape, split, -0.22, 0.18)
    return jnp.clip(spiked(result, jax.random.fold_in(own_key, 3), *heavy), -reach, reach).astype(kind)


def setup_inputs(seed: int = 0, part: int = 0) -> dict:
    seeds = jax.random.split(jax.random.key(seed), 4)
    part_keys = jax.random.split(jax.random.fold_in(seeds[3], part), 4)
    hidden = scatter_about(part_keys[0], (ROWS, FF), 1.0, 6.0, ((1, 16),))
    down_weight = heavy_noise(seeds[1], (FF, D), FF ** -0.5, 0.0546875, ((0, 16),), (0, 1, 16, 2.0))
    residual = scatter_about(part_keys[2], (ROWS, D), 1.0, 6.0, ((1, 16),))
    return dict(hidden=hidden, down_weight=down_weight, residual=residual)


def encode(values):
    row_count = values.shape[0]
    width = values.shape[1]
    blocks = values.reshape(row_count, width // BLOCK, BLOCK)
    scale = (jnp.max(jnp.abs(blocks), axis=2) + 1e-6).astype(jnp.bfloat16)
    coded = (blocks / scale.astype(jnp.float32)[:, :, None]).astype(jnp.bfloat16)
    return coded.reshape(row_count, width), scale


def decode(coded, scale):
    row_count = coded.shape[0]
    width = coded.shape[1]
    blocks = coded.astype(jnp.float32).reshape(row_count, width // BLOCK, BLOCK)
    return (blocks * scale.astype(jnp.float32)[:, :, None]).reshape(row_count, width)


def reference(hidden, down_weight, residual):
    group_width = FF // N_TP

    def add_group(total, group):
        start = (group * group_width).astype(jnp.int32)
        part_hidden = lax.dynamic_slice_in_dim(hidden, start, group_width, 1)
        part_weight = lax.dynamic_slice_in_dim(down_weight, start, group_width, 0)
        term = jnp.dot(part_hidden, part_weight, preferred_element_type=jnp.float32)
        coded, scale = encode(term)
        return total + decode(coded, scale), None

    summed, unused = lax.scan(add_group, residual.astype(jnp.float32), jnp.arange(N_TP, dtype=jnp.int32))
    out_values, out_scales = encode(summed)
    return (out_values, out_scales)
```

```python
import functools

import jax
import jax.numpy as jnp
from jax import lax
from jax.experimental import pallas as pl
from jax.experimental.pallas import tpu as pltpu
from jax.sharding import PartitionSpec as P

BLOCK = 128
MESH = pl.DeviceIdType.MESH
BF16 = jnp.bfloat16
F32 = jnp.float32
SLOTS = 16


def factor(count):
    chips = count // 2
    x = 1 << ((chips.bit_length() - 1) // 3)
    return chips // x, x


def kernel(
    n, h_hbm, w_hbm, res_ref, out_ref, osc_ref,
    h_ref, wbuf, a_send, a_recv, a_acc, b_send, b_recv, b_acc, c_send, c_recv, c_acc,
    g_ref, sc_acc, sz, sx, sk, h_sem, w_sem,
    sa, ra, sb, rb, sc, rc, sgz, rgz, sgx, rgx, sgk, rgk, ssz, rsz, ssx, rsx, ssk, rsk,
):
    zs, xs = factor(n)
    half = zs * xs
    chunks = g_ref.shape[0]
    rows, w = g_ref.shape[4], g_ref.shape[5]
    cols = chunks * w
    total = chunks * n
    slots = wbuf.shape[0]
    me = lax.axis_index("tp")
    mk, mx, mz = lax.rem(me, 2), lax.rem(me // 2, xs), me // (2 * xs)

    def device(z, x, k):
        return {"tp": (z * xs + x) * 2 + k}

    core_peer = device(mz, mx, 1 - mk)

    def x_peer(j):
        return lax.rem(mx + j + xs, xs)

    def z_peer(j):
        return lax.rem(mz + j + zs, zs)

    def w_copy(g):
        chunk, p = g // n, lax.rem(g, n)
        k = lax.rem(mk + 1 + p // half, 2)
        r = lax.rem(p, half)
        x, z = r // zs, lax.rem(r, zs)
        column = pl.multiple_of(((z * xs + x) * 2 + k) * cols + chunk * w, 128)
        slot = lax.rem(g, slots)
        return pltpu.make_async_copy(w_hbm.at[:, pl.ds(column, w)], wbuf.at[slot], w_sem.at[slot])

    def remote(src, dst, send, recv, dev):
        return pltpu.make_async_remote_copy(
            src_ref=src, dst_ref=dst, send_sem=send, recv_sem=recv, device_id=dev, device_id_type=MESH
        )

    h_copy = pltpu.make_async_copy(h_hbm, h_ref, h_sem)
    h_copy.start()

    def prime(g, carry):
        w_copy(g).start()
        return carry

    lax.fori_loop(0, min(slots, total), prime, 0)

    barrier = pltpu.get_barrier_semaphore()
    peers = [core_peer]
    peers += [device(mz, x_peer(j), mk) for j in range(1, xs)]
    peers += [device(z_peer(j), mx, mk) for j in range(1, zs)]
    for peer in peers:
        pl.semaphore_signal(barrier, inc=1, device_id=peer, device_id_type=MESH)
    sc_acc[...] = jnp.zeros_like(sc_acc)
    h_copy.wait()

    def multiply(c, start, stop, store):
        def body(p, carry):
            g = c * n + p
            w_copy(g).wait()
            term = jnp.dot(h_ref[...], wbuf[lax.rem(g, slots)], preferred_element_type=F32)
            store(lax.rem(p, half), term)

            @pl.when(g + slots < total)
            def _():
                w_copy(g + slots).start()

            return carry

        lax.fori_loop(start, stop, body, 0)

    def to_send(c):
        def store(r, term):
            a_send[c, r // zs, lax.rem(r, zs)] = term.astype(BF16)

        return store

    def to_keep(c):
        def store(r, term):
            a_acc[r // zs, lax.rem(r, zs)] = term

        return store

    def core_copy(c):
        return remote(a_send.at[c], a_recv.at[c], sa.at[c], ra.at[c], core_peer)

    def x_copy(c, j):
        return remote(b_send.at[c, j - 1], b_recv.at[c, j - 1], sb.at[c, j - 1], rb.at[c, j - 1], device(mz, x_peer(j), mk))

    def z_copy(c, j):
        return remote(c_send.at[c, j - 1], c_recv.at[c, j - 1], sc.at[c, j - 1], rc.at[c, j - 1], device(z_peer(j), mx, mk))

    def gz_copy(c, j, z):
        part = g_ref.at[c, mk, mx, z]
        return remote(part, part, sgz.at[c, j - 1], rgz.at[c, j - 1], device(z_peer(j), mx, mk))

    def gx_copy(c, j, x):
        part = g_ref.at[c, mk, x]
        return remote(part, part, sgx.at[c, j - 1], rgx.at[c, j - 1], device(mz, x_peer(j), mk))

    def gk_copy(c, k):
        part = g_ref.at[c, k]
        return remote(part, part, sgk.at[c], rgk.at[c], core_peer)

    def sz_copy(j):
        return remote(sz.at[0], sz.at[j], ssz.at[j - 1], rsz.at[j - 1], device(z_peer(j), mx, mk))

    def sx_copy(j):
        return remote(sx.at[0], sx.at[j], ssx.at[j - 1], rsx.at[j - 1], device(mz, x_peer(j), mk))

    def sk_copy():
        return remote(sk.at[0], sk.at[1], ssk, rsk, core_peer)

    def gathered(buf, count):
        value = buf[0].astype(F32)
        for j in range(1, count):
            value = value + buf[j].astype(F32)
        return value.astype(BF16)

    def reduce_core(c):
        core_copy(c).wait_recv()
        for j in range(1, xs):
            x = x_peer(j)
            b_send[c, j - 1] = (a_acc[x] + a_recv[c, x].astype(F32)).astype(BF16)
            x_copy(c, j).start()
        b_acc[c] = a_acc[mx] + a_recv[c, mx].astype(F32)

    def reduce_x(c):
        for j in range(1, xs):
            x_copy(c, j).wait_recv()

        def part(z):
            value = b_acc[c, z]
            for j in range(1, xs):
                value = value + b_recv[c, j - 1, z].astype(F32)
            return value

        for j in range(1, zs):
            c_send[c, j - 1] = part(z_peer(j)).astype(BF16)
            z_copy(c, j).start()
        c_acc[c] = part(mz) + res_ref[:, c * w:(c + 1) * w].astype(F32)

    def reduce_z(c):
        for j in range(1, zs):
            z_copy(c, j).wait_recv()
        summed = c_acc[c]
        for j in range(1, zs):
            summed = summed + c_recv[c, j - 1].astype(F32)
        lane = lax.broadcasted_iota(jnp.int32, sc_acc.shape, 1)
        first = (me * cols + c * w) // BLOCK
        for b in range(w // BLOCK):
            block = summed[:, b * BLOCK:(b + 1) * BLOCK]
            scale = (jnp.max(jnp.abs(block), axis=1, keepdims=True) + 1e-6).astype(BF16).astype(F32)
            g_ref[c, mk, mx, mz, :, b * BLOCK:(b + 1) * BLOCK] = (block / scale).astype(BF16)
            sc_acc[...] = jnp.where(lane == first + b, scale, sc_acc[...])
        for j in range(1, zs):
            gz_copy(c, j, mz).start()
        if c == chunks - 1:
            sz[0] = sc_acc[...].astype(BF16)
            for j in range(1, zs):
                sz_copy(j).start()

    def gather_x(c):
        for j in range(1, zs):
            gz_copy(c, j, z_peer(-j)).wait_recv()
        for j in range(1, xs):
            gx_copy(c, j, mx).start()
        if c == chunks - 1:
            for j in range(1, zs):
                sz_copy(j).wait_recv()
            sx[0] = gathered(sz, zs)
            for j in range(1, xs):
                sx_copy(j).start()

    def gather_core(c):
        for j in range(1, xs):
            gx_copy(c, j, x_peer(-j)).wait_recv()
        gk_copy(c, mk).start()
        if c == chunks - 1:
            for j in range(1, xs):
                sx_copy(j).wait_recv()
            sk[0] = gathered(sx, xs)
            sk_copy().start()

    def finish(c):
        gk_copy(c, 1 - mk).wait_recv()
        for k in range(2):
            for x in range(xs):
                for z in range(zs):
                    column = ((z * xs + x) * 2 + k) * cols + c * w
                    out_ref[:, column:column + w] = g_ref[c, k, x, z]
        if c == chunks - 1:
            sk_copy().wait_recv()
            osc_ref[...] = gathered(sk, 2)

    quarter = half // 2
    later = [[] for _ in range(4 * chunks + 16)]
    steps = ((0, reduce_core), (2, reduce_x), (4, reduce_z), (6, gather_x), (8, gather_core), (10, finish))
    for c in range(chunks):
        for delay, step in steps:
            later[4 * c + 3 + delay].append((step, c))
    for t in range(4 * chunks + 16):
        if t < 4 * chunks:
            c, q = t // 4, t % 4
            multiply(c, q * quarter, (q + 1) * quarter, to_send(c) if q < 2 else to_keep(c))
            if q == 1:
                if c == 0:
                    pl.semaphore_wait(barrier, len(peers))
                core_copy(c).start()
        for step, c in later[t]:
            step(c)

    for c in range(chunks):
        core_copy(c).wait_send()
        gk_copy(c, mk).wait_send()
        for j in range(1, xs):
            x_copy(c, j).wait_send()
            gx_copy(c, j, mx).wait_send()
        for j in range(1, zs):
            z_copy(c, j).wait_send()
            gz_copy(c, j, mz).wait_send()
    for j in range(1, zs):
        sz_copy(j).wait_send()
    for j in range(1, xs):
        sx_copy(j).wait_send()
    sk_copy().wait_send()


def shards(hidden, down_weight, residual):
    n = lax.axis_size("tp")
    zs, xs = factor(n)
    rows, depth = hidden.shape
    width = down_weight.shape[1]
    cols = width // n
    w = min(256, cols)
    chunks = cols // w
    dma = pltpu.SemaphoreType.DMA
    vmem = pltpu.VMEM
    scratch = [
        vmem((rows, depth), BF16),
        vmem((SLOTS, depth, w), BF16),
        vmem((chunks, xs, zs, rows, w), BF16),
        vmem((chunks, xs, zs, rows, w), BF16),
        vmem((xs, zs, rows, w), F32),
        vmem((chunks, xs - 1, zs, rows, w), BF16),
        vmem((chunks, xs - 1, zs, rows, w), BF16),
        vmem((chunks, zs, rows, w), F32),
        vmem((chunks, zs - 1, rows, w), BF16),
        vmem((chunks, zs - 1, rows, w), BF16),
        vmem((chunks, rows, w), F32),
        vmem((chunks, 2, xs, zs, rows, w), BF16),
        vmem((rows, width // BLOCK), F32),
        vmem((zs, rows, width // BLOCK), BF16),
        vmem((xs, rows, width // BLOCK), BF16),
        vmem((2, rows, width // BLOCK), BF16),
        dma, dma((SLOTS,)),
        dma((chunks,)), dma((chunks,)),
        dma((chunks, xs - 1)), dma((chunks, xs - 1)),
        dma((chunks, zs - 1)), dma((chunks, zs - 1)),
        dma((chunks, zs - 1)), dma((chunks, zs - 1)),
        dma((chunks, xs - 1)), dma((chunks, xs - 1)),
        dma((chunks,)), dma((chunks,)),
        dma((zs - 1,)), dma((zs - 1,)),
        dma((xs - 1,)), dma((xs - 1,)),
        dma, dma,
    ]
    hbm = pl.BlockSpec(memory_space=pl.ANY)
    whole = pl.BlockSpec(memory_space=pltpu.VMEM)
    return pl.pallas_call(
        functools.partial(kernel, n),
        out_shape=(
            jax.ShapeDtypeStruct((rows, width), BF16),
            jax.ShapeDtypeStruct((rows, width // BLOCK), BF16),
        ),
        in_specs=[hbm, hbm, whole],
        out_specs=(whole, whole),
        scratch_shapes=scratch,
        compiler_params=pltpu.CompilerParams(collective_id=0, has_side_effects=True, vmem_limit_bytes=48 * 2**20),
        cost_estimate=pl.CostEstimate(
            flops=2 * rows * depth * width, bytes_accessed=2 * depth * width, transcendentals=0
        ),
    )(hidden, down_weight, residual)


def solution(mesh):
    in_specs = (P("groups", "tp"), P("tp", None), P("groups", "tp"))
    out_specs = (P("groups", None), P("groups", None))
    return jax.shard_map(shards, mesh=mesh, in_specs=in_specs, out_specs=out_specs, check_vma=False)
```

```python
import functools

import jax
import jax.numpy as jnp
from jax import lax
from jax.experimental import pallas as pl
from jax.experimental.pallas import tpu as pltpu
from jax.sharding import PartitionSpec as P

BLOCK = 128
MESH = pl.DeviceIdType.MESH
BF16 = jnp.bfloat16
F32 = jnp.float32
SLOTS = 16
DIRECT = 2
WIDE_DELAYS = (0, 3, 6, 9, 12, 13)
NARROW_DELAYS = (0, 3.6, 7.2, 8.2)


def factor(count):
    chips = count // 2
    x = 1 << ((chips.bit_length() - 1) // 3)
    return chips // x, x


def plan(cols, n):
    narrow = DIRECT if cols >= 4 * BLOCK and n <= 32 else 0
    wide = min(2 * BLOCK, cols)
    return (cols - narrow * BLOCK) // wide, wide, narrow


class Refs:
    def __init__(self, names, refs):
        for name, ref in zip(names, refs):
            setattr(self, name, ref)


def kernel(n, names, h_hbm, w_hbm, res_ref, out_ref, osc_ref, *scratch):
    s = Refs(names, scratch)
    zs, xs = factor(n)
    half = zs * xs
    rows, cols = res_ref.shape
    wides, wide, narrows = plan(cols, n)
    chunks = wides + narrows
    slot_w = s.wbuf.shape[2]
    per_wide = slot_w // wide
    wide_items = wides * n // per_wide
    total = wide_items + narrows * n * BLOCK // slot_w
    slots = s.wbuf.shape[0]
    me = lax.axis_index("tp")
    mk, mx, mz = lax.rem(me, 2), lax.rem(me // 2, xs), me // (2 * xs)
    chip = me // 2

    def device(z, x, k):
        return {"tp": (z * xs + x) * 2 + k}

    core_peer = device(mz, mx, 1 - mk)

    def x_peer(j):
        return lax.rem(mx + j + xs, xs)

    def z_peer(j):
        return lax.rem(mz + j + zs, zs)

    def chip_peer(j):
        return lax.rem(chip + j + half, half)

    def item_copies(g, first, offset, w):
        pieces = slot_w // w
        items = n // pieces
        chunk, p = (g - first) // items, lax.rem(g - first, items)
        k = lax.rem(mk + 1 + p // (items // 2), 2)
        r = lax.rem(p, items // 2) * pieces
        x, z = r // zs, lax.rem(r, zs)
        slot = lax.rem(g, slots)
        copies = []
        for i in range(pieces):
            column = pl.multiple_of(((((z + i) * xs + x) * 2 + k) * cols + offset) + chunk * w, BLOCK)
            copies.append(
                pltpu.make_async_copy(
                    w_hbm.at[:, pl.ds(column, w)], s.wbuf.at[slot, :, pl.ds(i * w, w)], s.w_sem.at[slot, i]
                )
            )
        return copies

    def wide_copies(g):
        return item_copies(g, 0, 0, wide)

    def narrow_copies(g):
        return item_copies(g, wide_items, wides * wide, BLOCK)

    def start_item(g):
        @pl.when(g < wide_items)
        def _():
            for copy in wide_copies(g):
                copy.start()

        if narrows:
            @pl.when(jnp.logical_and(g >= wide_items, g < total))
            def _():
                for copy in narrow_copies(g):
                    copy.start()

    def remote(src, dst, send, recv, dev):
        return pltpu.make_async_remote_copy(
            src_ref=src, dst_ref=dst, send_sem=send, recv_sem=recv, device_id=dev, device_id_type=MESH
        )

    h_copy = pltpu.make_async_copy(h_hbm, s.h, s.h_sem)
    h_copy.start()

    def prime(g, carry):
        start_item(g)
        return carry

    lax.fori_loop(0, min(slots, total), prime, 0)

    barrier = pltpu.get_barrier_semaphore()
    peers = [core_peer]
    if narrows:
        peers += [{"tp": chip_peer(j) * 2 + mk} for j in range(1, half)]
    else:
        peers += [device(mz, x_peer(j), mk) for j in range(1, xs)]
        peers += [device(z_peer(j), mx, mk) for j in range(1, zs)]
    for peer in peers:
        pl.semaphore_signal(barrier, inc=1, device_id=peer, device_id_type=MESH)
    s.sc_acc[...] = jnp.zeros_like(s.sc_acc)
    h_copy.wait()

    def multiply(first, start, stop, copies, store):
        def body(p, carry):
            g = first + p
            for copy in copies(g):
                copy.wait()
            term = jnp.dot(s.h[...], s.wbuf[lax.rem(g, slots)], preferred_element_type=F32)
            store(p, term)
            start_item(g + slots)
            return carry

        lax.fori_loop(start, stop, body, 0, unroll=min(4, stop - start))

    def storing(ref, w, kind):
        pieces = slot_w // w
        items = n // pieces // 2

        def store(p, term):
            r = lax.rem(p, items) * pieces
            for i in range(pieces):
                ref[r // zs, lax.rem(r, zs) + i] = term[:, i * w:(i + 1) * w].astype(kind)

        return store

    def core_copy(c):
        return remote(s.a_send.at[c], s.a_recv.at[c], s.sa.at[c], s.ra.at[c], core_peer)

    def x_copy(c, j):
        return remote(s.b_send.at[c, j - 1], s.b_recv.at[c, j - 1], s.sb.at[c, j - 1], s.rb.at[c, j - 1], device(mz, x_peer(j), mk))

    def z_copy(c, j):
        return remote(s.c_send.at[c, j - 1], s.c_recv.at[c, j - 1], s.sc.at[c, j - 1], s.rc.at[c, j - 1], device(z_peer(j), mx, mk))

    def gz_copy(c, j, z):
        part = s.g.at[c, mk, mx, z]
        return remote(part, part, s.sgz.at[c, j - 1], s.rgz.at[c, j - 1], device(z_peer(j), mx, mk))

    def gx_copy(c, j, x):
        part = s.g.at[c, mk, x]
        return remote(part, part, s.sgx.at[c, j - 1], s.rgx.at[c, j - 1], device(mz, x_peer(j), mk))

    def gk_copy(c, k):
        part = s.g.at[c, k]
        return remote(part, part, s.sgk.at[c], s.rgk.at[c], core_peer)

    def d_core_copy(c):
        return remote(s.e_send.at[c], s.e_recv.at[c], s.se.at[c], s.re.at[c], core_peer)

    def d_copy(c, j):
        return remote(s.d_send.at[c, j - 1], s.d_recv.at[c, j - 1], s.sd.at[c, j - 1], s.rd.at[c, j - 1], {"tp": chip_peer(j) * 2 + mk})

    def dg_copy(c, j, owner):
        part = s.dg.at[c, mk, lax.rem(owner, xs), owner // xs]
        return remote(part, part, s.sdg.at[c, j - 1], s.rdg.at[c, j - 1], {"tp": chip_peer(j) * 2 + mk})

    def dgk_copy(c, k):
        part = s.dg.at[c, k]
        return remote(part, part, s.sdk.at[c], s.rdk.at[c], core_peer)

    def sz_copy(j):
        return remote(s.sz.at[0], s.sz.at[j], s.ssz.at[j - 1], s.rsz.at[j - 1], device(z_peer(j), mx, mk))

    def sx_copy(j):
        return remote(s.sx.at[0], s.sx.at[j], s.ssx.at[j - 1], s.rsx.at[j - 1], device(mz, x_peer(j), mk))

    def sd_copy(j):
        return remote(s.sd_buf.at[0], s.sd_buf.at[j], s.ssd.at[j - 1], s.rsd.at[j - 1], {"tp": chip_peer(j) * 2 + mk})

    def sk_copy():
        return remote(s.sk.at[0], s.sk.at[1], s.ssk, s.rsk, core_peer)

    def gathered(buf, count):
        value = buf[0].astype(F32)
        for j in range(1, count):
            value = value + buf[j].astype(F32)
        return value.astype(BF16)

    def encode(summed, offset, out):
        lane = lax.broadcasted_iota(jnp.int32, s.sc_acc.shape, 1)
        first = (me * cols + offset) // BLOCK
        for b in range(summed.shape[1] // BLOCK):
            block = summed[:, b * BLOCK:(b + 1) * BLOCK]
            scale = (jnp.max(jnp.abs(block), axis=1, keepdims=True) + 1e-6).astype(BF16).astype(F32)
            out[:, b * BLOCK:(b + 1) * BLOCK] = (block / scale).astype(BF16)
            s.sc_acc[...] = jnp.where(lane == first + b, scale, s.sc_acc[...])

    def write_out(part, k, offset, w):
        for x in range(xs):
            for z in range(zs):
                column = ((z * xs + x) * 2 + k) * cols + offset
                out_ref[:, column:column + w] = part[k, x, z]

    def reduce_core(c):
        core_copy(c).wait_recv()
        for j in range(1, xs):
            x = x_peer(j)
            s.b_send[c, j - 1] = (s.a_acc[x] + s.a_recv[c, x].astype(F32)).astype(BF16)
            x_copy(c, j).start()
        s.b_acc[c] = s.a_acc[mx] + s.a_recv[c, mx].astype(F32)

    def reduce_x(c):
        for j in range(1, xs):
            x_copy(c, j).wait_recv()

        def part(z):
            value = s.b_acc[c, z]
            for j in range(1, xs):
                value = value + s.b_recv[c, j - 1, z].astype(F32)
            return value

        for j in range(1, zs):
            s.c_send[c, j - 1] = part(z_peer(j)).astype(BF16)
            z_copy(c, j).start()
        s.c_acc[c] = part(mz) + res_ref[:, c * wide:(c + 1) * wide].astype(F32)

    def reduce_z(c):
        for j in range(1, zs):
            z_copy(c, j).wait_recv()
        summed = s.c_acc[c]
        for j in range(1, zs):
            summed = summed + s.c_recv[c, j - 1].astype(F32)
        encode(summed, c * wide, s.g.at[c, mk, mx, mz])
        for j in range(1, zs):
            gz_copy(c, j, mz).start()
        if c == chunks - 1:
            s.sz[0] = s.sc_acc[...].astype(BF16)
            for j in range(1, zs):
                sz_copy(j).start()

    def gather_x(c):
        for j in range(1, zs):
            gz_copy(c, j, z_peer(-j)).wait_recv()
        for j in range(1, xs):
            gx_copy(c, j, mx).start()
        if c == chunks - 1:
            for j in range(1, zs):
                sz_copy(j).wait_recv()
            s.sx[0] = gathered(s.sz, zs)
            for j in range(1, xs):
                sx_copy(j).start()

    def gather_core(c):
        for j in range(1, xs):
            gx_copy(c, j, x_peer(-j)).wait_recv()
        gk_copy(c, mk).start()
        if c == chunks - 1:
            for j in range(1, xs):
                sx_copy(j).wait_recv()
            s.sk[0] = gathered(s.sx, xs)
            sk_copy().start()

    def finish(c):
        gk_copy(c, 1 - mk).wait_recv()
        for k in range(2):
            write_out(s.g.at[c], k, c * wide, wide)
        if c == chunks - 1:
            sk_copy().wait_recv()
            osc_ref[...] = gathered(s.sk, 2)

    def narrow_at(c):
        return wides * wide + c * BLOCK

    def d_reduce_core(c):
        d_core_copy(c).wait_recv()
        for j in range(1, half):
            q = chip_peer(j)
            x, z = lax.rem(q, xs), q // xs
            s.d_send[c, j - 1] = (s.e_acc[x, z] + s.e_recv[c, x, z].astype(F32)).astype(BF16)
            d_copy(c, j).start()
        at = narrow_at(c)
        s.d_acc[c] = s.e_acc[mx, mz] + s.e_recv[c, mx, mz].astype(F32) + res_ref[:, at:at + BLOCK].astype(F32)

    def d_reduce(c):
        for j in range(1, half):
            d_copy(c, j).wait_recv()
        summed = s.d_acc[c]
        for j in range(1, half):
            summed = summed + s.d_recv[c, j - 1].astype(F32)
        encode(summed, narrow_at(c), s.dg.at[c, mk, mx, mz])
        for j in range(1, half):
            dg_copy(c, j, chip).start()
        if c == narrows - 1:
            s.sd_buf[0] = s.sc_acc[...].astype(BF16)
            for j in range(1, half):
                sd_copy(j).start()

    def d_gather_core(c):
        for j in range(1, half):
            dg_copy(c, j, chip_peer(-j)).wait_recv()
        dgk_copy(c, mk).start()
        if c == narrows - 1:
            for j in range(1, half):
                sd_copy(j).wait_recv()
            s.sk[0] = gathered(s.sd_buf, half)
            sk_copy().start()

    def d_finish(c):
        dgk_copy(c, 1 - mk).wait_recv()
        for k in range(2):
            write_out(s.dg.at[c], k, narrow_at(c), BLOCK)
        if c == narrows - 1:
            sk_copy().wait_recv()
            osc_ref[...] = gathered(s.sk, 2)

    line = []

    def matmul_unit(first, start, stop, copies, store):
        return lambda: multiply(first, start, stop, copies, store)

    def send_core(copy, c, opening):
        def step():
            if opening:
                pl.semaphore_wait(barrier, len(peers))
            copy(c).start()

        return step

    for c in range(wides):
        items = n // per_wide
        for q in range(4):
            store = storing(s.a_send.at[c], wide, BF16) if q < 2 else storing(s.a_acc, wide, F32)
            unit = matmul_unit(c * items, q * items // 4, (q + 1) * items // 4, wide_copies, store)
            line.append((4 * c + q, 0, unit))
        line.append((4 * c + 1, 1, send_core(core_copy, c, c == 0)))
        for order, (delay, step) in enumerate(zip(WIDE_DELAYS, (reduce_core, reduce_x, reduce_z, gather_x, gather_core, finish))):
            line.append((4 * c + 3 + delay, 2 + order, functools.partial(step, c)))
    for c in range(narrows):
        items = n * BLOCK // slot_w
        for q in range(2):
            store = storing(s.e_send.at[c], BLOCK, BF16) if q < 1 else storing(s.e_acc, BLOCK, F32)
            unit = matmul_unit(wide_items + c * items, q * items // 2, (q + 1) * items // 2, narrow_copies, store)
            line.append((4 * wides + 2 * c + q, 0, unit))
        line.append((4 * wides + 2 * c, 1, send_core(d_core_copy, c, False)))
        for order, (delay, step) in enumerate(zip(NARROW_DELAYS, (d_reduce_core, d_reduce, d_gather_core, d_finish))):
            line.append((4 * wides + 2 * c + 1 + delay, 2 + order, functools.partial(step, c)))
    for time, order, step in sorted(line, key=lambda entry: entry[:2]):
        step()

    for c in range(wides):
        core_copy(c).wait_send()
        gk_copy(c, mk).wait_send()
        for j in range(1, xs):
            x_copy(c, j).wait_send()
            gx_copy(c, j, mx).wait_send()
        for j in range(1, zs):
            z_copy(c, j).wait_send()
            gz_copy(c, j, mz).wait_send()
    for c in range(narrows):
        d_core_copy(c).wait_send()
        dgk_copy(c, mk).wait_send()
        for j in range(1, half):
            d_copy(c, j).wait_send()
            dg_copy(c, j, chip).wait_send()
    if narrows:
        for j in range(1, half):
            sd_copy(j).wait_send()
    else:
        for j in range(1, zs):
            sz_copy(j).wait_send()
        for j in range(1, xs):
            sx_copy(j).wait_send()
    sk_copy().wait_send()


def shards(hidden, down_weight, residual):
    n = lax.axis_size("tp")
    zs, xs = factor(n)
    half = zs * xs
    rows, depth = hidden.shape
    width = down_weight.shape[1]
    cols = width // n
    wides, w, narrows = plan(cols, n)
    dma = pltpu.SemaphoreType.DMA
    vmem = pltpu.VMEM
    scales = (rows, width // BLOCK)
    scratch = {
        "h": vmem((rows, depth), BF16),
        "h_sem": dma,
        "wbuf": vmem((SLOTS, depth, 2 * BLOCK), BF16),
        "w_sem": dma((SLOTS, 2)),
        "a_send": vmem((wides, xs, zs, rows, w), BF16),
        "a_recv": vmem((wides, xs, zs, rows, w), BF16),
        "a_acc": vmem((xs, zs, rows, w), F32),
        "b_send": vmem((wides, xs - 1, zs, rows, w), BF16),
        "b_recv": vmem((wides, xs - 1, zs, rows, w), BF16),
        "b_acc": vmem((wides, zs, rows, w), F32),
        "c_send": vmem((wides, zs - 1, rows, w), BF16),
        "c_recv": vmem((wides, zs - 1, rows, w), BF16),
        "c_acc": vmem((wides, rows, w), F32),
        "g": vmem((wides, 2, xs, zs, rows, w), BF16),
        "sc_acc": vmem(scales, F32),
        "sk": vmem((2,) + scales, BF16),
        "ssk": dma,
        "rsk": dma,
    }
    for name, shape in (("a", ()), ("b", (xs - 1,)), ("c", (zs - 1,)), ("gz", (zs - 1,)), ("gx", (xs - 1,)), ("gk", ())):
        scratch["s" + name] = dma((wides,) + shape)
        scratch["r" + name] = dma((wides,) + shape)
    if narrows:
        scratch.update({
            "e_send": vmem((narrows, xs, zs, rows, BLOCK), BF16),
            "e_recv": vmem((narrows, xs, zs, rows, BLOCK), BF16),
            "e_acc": vmem((xs, zs, rows, BLOCK), F32),
            "d_send": vmem((narrows, half - 1, rows, BLOCK), BF16),
            "d_recv": vmem((narrows, half - 1, rows, BLOCK), BF16),
            "d_acc": vmem((narrows, rows, BLOCK), F32),
            "dg": vmem((narrows, 2, xs, zs, rows, BLOCK), BF16),
            "sd_buf": vmem((half,) + scales, BF16),
            "ssd": dma((half - 1,)),
            "rsd": dma((half - 1,)),
        })
        for name, shape in (("e", ()), ("d", (half - 1,)), ("dg", (half - 1,)), ("dk", ())):
            scratch["s" + name] = dma((narrows,) + shape)
            scratch["r" + name] = dma((narrows,) + shape)
    else:
        scratch.update({
            "sz": vmem((zs,) + scales, BF16),
            "sx": vmem((xs,) + scales, BF16),
            "ssz": dma((zs - 1,)),
            "rsz": dma((zs - 1,)),
            "ssx": dma((xs - 1,)),
            "rsx": dma((xs - 1,)),
        })
    hbm = pl.BlockSpec(memory_space=pl.ANY)
    whole = pl.BlockSpec(memory_space=pltpu.VMEM)
    return pl.pallas_call(
        functools.partial(kernel, n, tuple(scratch)),
        out_shape=(
            jax.ShapeDtypeStruct((rows, width), BF16),
            jax.ShapeDtypeStruct(scales, BF16),
        ),
        in_specs=[hbm, hbm, whole],
        out_specs=(whole, whole),
        scratch_shapes=list(scratch.values()),
        compiler_params=pltpu.CompilerParams(collective_id=0, has_side_effects=True, vmem_limit_bytes=48 * 2**20),
        cost_estimate=pl.CostEstimate(
            flops=2 * rows * depth * width, bytes_accessed=2 * depth * width, transcendentals=0
        ),
    )(hidden, down_weight, residual)


def solution(mesh):
    in_specs = (P("groups", "tp"), P("tp", None), P("groups", "tp"))
    out_specs = (P("groups", None), P("groups", None))
    return jax.shard_map(shards, mesh=mesh, in_specs=in_specs, out_specs=out_specs, check_vma=False)
```

```python
import functools

import jax
import jax.numpy as jnp
from jax import lax
from jax.experimental import pallas as pl
from jax.experimental.pallas import tpu as pltpu
from jax.sharding import PartitionSpec as P

BLOCK = 128
MESH = pl.DeviceIdType.MESH
BF16 = jnp.bfloat16
F32 = jnp.float32
SLOTS = 16
DIRECT = 4
WIDE_DELAYS = (0, 3, 6, 9, 12, 13)
NARROW_DELAYS = (0, 3.6, 7.2, 8.2)


def factor(count):
    chips = count // 2
    x = 1 << ((chips.bit_length() - 1) // 3)
    return chips // x, x


def plan(cols, n):
    narrow = DIRECT if cols >= 4 * BLOCK and n <= 32 else 0
    wide = min(2 * BLOCK, cols)
    return (cols - narrow * BLOCK) // wide, wide, narrow


class Refs:
    def __init__(self, names, refs):
        for name, ref in zip(names, refs):
            setattr(self, name, ref)


def kernel(n, names, h_hbm, w_hbm, res_ref, out_ref, osc_ref, *scratch):
    s = Refs(names, scratch)
    zs, xs = factor(n)
    half = zs * xs
    rows, cols = res_ref.shape
    wides, wide, narrows = plan(cols, n)
    chunks = wides + narrows
    slot_w = s.wbuf.shape[2]
    per_wide = slot_w // wide
    wide_items = wides * n // per_wide
    total = wide_items + narrows * n * BLOCK // slot_w
    slots = s.wbuf.shape[0]
    me = lax.axis_index("tp")
    mk, mx, mz = lax.rem(me, 2), lax.rem(me // 2, xs), me // (2 * xs)
    chip = me // 2

    def device(z, x, k):
        return {"tp": (z * xs + x) * 2 + k}

    core_peer = device(mz, mx, 1 - mk)

    def x_peer(j):
        return lax.rem(mx + j + xs, xs)

    def z_peer(j):
        return lax.rem(mz + j + zs, zs)

    def chip_peer(j):
        return lax.rem(chip + j + half, half)

    def item_copies(g, first, offset, w):
        pieces = slot_w // w
        items = n // pieces
        chunk, p = (g - first) // items, lax.rem(g - first, items)
        k = lax.rem(mk + 1 + p // (items // 2), 2)
        r = lax.rem(p, items // 2) * pieces
        x, z = r // zs, lax.rem(r, zs)
        slot = lax.rem(g, slots)
        copies = []
        for i in range(pieces):
            column = pl.multiple_of(((((z + i) * xs + x) * 2 + k) * cols + offset) + chunk * w, BLOCK)
            copies.append(
                pltpu.make_async_copy(
                    w_hbm.at[:, pl.ds(column, w)], s.wbuf.at[slot, :, pl.ds(i * w, w)], s.w_sem.at[slot, i]
                )
            )
        return copies

    def wide_copies(g):
        return item_copies(g, 0, 0, wide)

    def narrow_copies(g):
        return item_copies(g, wide_items, wides * wide, BLOCK)

    def start_item(g):
        @pl.when(g < wide_items)
        def _():
            for copy in wide_copies(g):
                copy.start()

        if narrows:
            @pl.when(jnp.logical_and(g >= wide_items, g < total))
            def _():
                for copy in narrow_copies(g):
                    copy.start()

    def remote(src, dst, send, recv, dev):
        return pltpu.make_async_remote_copy(
            src_ref=src, dst_ref=dst, send_sem=send, recv_sem=recv, device_id=dev, device_id_type=MESH
        )

    h_copy = pltpu.make_async_copy(h_hbm, s.h, s.h_sem)
    h_copy.start()

    def prime(g, carry):
        start_item(g)
        return carry

    lax.fori_loop(0, min(slots, total), prime, 0)

    barrier = pltpu.get_barrier_semaphore()
    peers = [core_peer]
    if narrows:
        peers += [{"tp": chip_peer(j) * 2 + mk} for j in range(1, half)]
    else:
        peers += [device(mz, x_peer(j), mk) for j in range(1, xs)]
        peers += [device(z_peer(j), mx, mk) for j in range(1, zs)]
    for peer in peers:
        pl.semaphore_signal(barrier, inc=1, device_id=peer, device_id_type=MESH)
    s.sc_acc[...] = jnp.zeros_like(s.sc_acc)
    h_copy.wait()

    def multiply(first, start, stop, copies, store):
        def body(p, carry):
            g = first + p
            for copy in copies(g):
                copy.wait()
            term = jnp.dot(s.h[...], s.wbuf[lax.rem(g, slots)], preferred_element_type=F32)
            store(p, term)
            start_item(g + slots)
            return carry

        lax.fori_loop(start, stop, body, 0, unroll=min(4, stop - start))

    def storing(ref, w, kind):
        pieces = slot_w // w
        items = n // pieces // 2

        def store(p, term):
            r = lax.rem(p, items) * pieces
            for i in range(pieces):
                ref[r // zs, lax.rem(r, zs) + i] = term[:, i * w:(i + 1) * w].astype(kind)

        return store

    def core_copy(c):
        return remote(s.a_send.at[c], s.a_recv.at[c], s.sa.at[c], s.ra.at[c], core_peer)

    def x_copy(c, j):
        return remote(s.b_send.at[c, j - 1], s.b_recv.at[c, j - 1], s.sb.at[c, j - 1], s.rb.at[c, j - 1], device(mz, x_peer(j), mk))

    def z_copy(c, j):
        return remote(s.c_send.at[c, j - 1], s.c_recv.at[c, j - 1], s.sc.at[c, j - 1], s.rc.at[c, j - 1], device(z_peer(j), mx, mk))

    def gz_copy(c, j, z):
        part = s.g.at[c, mk, mx, z]
        return remote(part, part, s.sgz.at[c, j - 1], s.rgz.at[c, j - 1], device(z_peer(j), mx, mk))

    def gx_copy(c, j, x):
        part = s.g.at[c, mk, x]
        return remote(part, part, s.sgx.at[c, j - 1], s.rgx.at[c, j - 1], device(mz, x_peer(j), mk))

    def gk_copy(c, k):
        part = s.g.at[c, k]
        return remote(part, part, s.sgk.at[c], s.rgk.at[c], core_peer)

    def d_core_copy(c):
        return remote(s.e_send.at[c], s.e_recv.at[c], s.se.at[c], s.re.at[c], core_peer)

    def d_copy(c, j):
        return remote(s.d_send.at[c, j - 1], s.d_recv.at[c, j - 1], s.sd.at[c, j - 1], s.rd.at[c, j - 1], {"tp": chip_peer(j) * 2 + mk})

    def dg_copy(c, j, owner):
        part = s.dg.at[c, mk, lax.rem(owner, xs), owner // xs]
        return remote(part, part, s.sdg.at[c, j - 1], s.rdg.at[c, j - 1], {"tp": chip_peer(j) * 2 + mk})

    def dgk_copy(c, k):
        part = s.dg.at[c, k]
        return remote(part, part, s.sdk.at[c], s.rdk.at[c], core_peer)

    def sz_copy(j):
        return remote(s.sz.at[0], s.sz.at[j], s.ssz.at[j - 1], s.rsz.at[j - 1], device(z_peer(j), mx, mk))

    def sx_copy(j):
        return remote(s.sx.at[0], s.sx.at[j], s.ssx.at[j - 1], s.rsx.at[j - 1], device(mz, x_peer(j), mk))

    def sd_copy(j):
        return remote(s.sd_buf.at[0], s.sd_buf.at[j], s.ssd.at[j - 1], s.rsd.at[j - 1], {"tp": chip_peer(j) * 2 + mk})

    def sk_copy():
        return remote(s.sk.at[0], s.sk.at[1], s.ssk, s.rsk, core_peer)

    def gathered(buf, count):
        value = buf[0].astype(F32)
        for j in range(1, count):
            value = value + buf[j].astype(F32)
        return value.astype(BF16)

    def encode(summed, offset, out):
        lane = lax.broadcasted_iota(jnp.int32, s.sc_acc.shape, 1)
        first = (me * cols + offset) // BLOCK
        for b in range(summed.shape[1] // BLOCK):
            block = summed[:, b * BLOCK:(b + 1) * BLOCK]
            scale = (jnp.max(jnp.abs(block), axis=1, keepdims=True) + 1e-6).astype(BF16).astype(F32)
            out[:, b * BLOCK:(b + 1) * BLOCK] = (block / scale).astype(BF16)
            s.sc_acc[...] = jnp.where(lane == first + b, scale, s.sc_acc[...])

    def write_out(part, k, offset, w):
        for x in range(xs):
            for z in range(zs):
                column = ((z * xs + x) * 2 + k) * cols + offset
                out_ref[:, column:column + w] = part[k, x, z]

    def reduce_core(c):
        core_copy(c).wait_recv()
        for j in range(1, xs):
            x = x_peer(j)
            s.b_send[c, j - 1] = (s.a_acc[x] + s.a_recv[c, x].astype(F32)).astype(BF16)
            x_copy(c, j).start()
        s.b_acc[c] = s.a_acc[mx] + s.a_recv[c, mx].astype(F32)

    def reduce_x(c):
        for j in range(1, xs):
            x_copy(c, j).wait_recv()

        def part(z):
            value = s.b_acc[c, z]
            for j in range(1, xs):
                value = value + s.b_recv[c, j - 1, z].astype(F32)
            return value

        for j in range(1, zs):
            s.c_send[c, j - 1] = part(z_peer(j)).astype(BF16)
            z_copy(c, j).start()
        s.c_acc[c] = part(mz) + res_ref[:, c * wide:(c + 1) * wide].astype(F32)

    def reduce_z(c):
        for j in range(1, zs):
            z_copy(c, j).wait_recv()
        summed = s.c_acc[c]
        for j in range(1, zs):
            summed = summed + s.c_recv[c, j - 1].astype(F32)
        encode(summed, c * wide, s.g.at[c, mk, mx, mz])
        for j in range(1, zs):
            gz_copy(c, j, mz).start()
        if c == chunks - 1:
            s.sz[0] = s.sc_acc[...].astype(BF16)
            for j in range(1, zs):
                sz_copy(j).start()

    def gather_x(c):
        for j in range(1, zs):
            gz_copy(c, j, z_peer(-j)).wait_recv()
        for j in range(1, xs):
            gx_copy(c, j, mx).start()
        if c == chunks - 1:
            for j in range(1, zs):
                sz_copy(j).wait_recv()
            s.sx[0] = gathered(s.sz, zs)
            for j in range(1, xs):
                sx_copy(j).start()

    def gather_core(c):
        for j in range(1, xs):
            gx_copy(c, j, x_peer(-j)).wait_recv()
        gk_copy(c, mk).start()
        if c == chunks - 1:
            for j in range(1, xs):
                sx_copy(j).wait_recv()
            s.sk[0] = gathered(s.sx, xs)
            sk_copy().start()

    def finish(c):
        gk_copy(c, 1 - mk).wait_recv()
        for k in range(2):
            write_out(s.g.at[c], k, c * wide, wide)
        if c == chunks - 1:
            sk_copy().wait_recv()
            osc_ref[...] = gathered(s.sk, 2)

    def narrow_at(c):
        return wides * wide + c * BLOCK

    def d_reduce_core(c):
        d_core_copy(c).wait_recv()
        for j in range(1, half):
            q = chip_peer(j)
            x, z = lax.rem(q, xs), q // xs
            s.d_send[c, j - 1] = (s.e_acc[x, z] + s.e_recv[c, x, z].astype(F32)).astype(BF16)
            d_copy(c, j).start()
        at = narrow_at(c)
        s.d_acc[c] = s.e_acc[mx, mz] + s.e_recv[c, mx, mz].astype(F32) + res_ref[:, at:at + BLOCK].astype(F32)

    def d_reduce(c):
        for j in range(1, half):
            d_copy(c, j).wait_recv()
        summed = s.d_acc[c]
        for j in range(1, half):
            summed = summed + s.d_recv[c, j - 1].astype(F32)
        encode(summed, narrow_at(c), s.dg.at[c, mk, mx, mz])
        for j in range(1, half):
            dg_copy(c, j, chip).start()
        if c == narrows - 1:
            s.sd_buf[0] = s.sc_acc[...].astype(BF16)
            for j in range(1, half):
                sd_copy(j).start()

    def d_gather_core(c):
        for j in range(1, half):
            dg_copy(c, j, chip_peer(-j)).wait_recv()
        dgk_copy(c, mk).start()
        if c == narrows - 1:
            for j in range(1, half):
                sd_copy(j).wait_recv()
            s.sk[0] = gathered(s.sd_buf, half)
            sk_copy().start()

    def d_finish(c):
        dgk_copy(c, 1 - mk).wait_recv()
        for k in range(2):
            write_out(s.dg.at[c], k, narrow_at(c), BLOCK)
        if c == narrows - 1:
            sk_copy().wait_recv()
            osc_ref[...] = gathered(s.sk, 2)

    line = []

    def matmul_unit(first, start, stop, copies, store):
        return lambda: multiply(first, start, stop, copies, store)

    def send_core(copy, c, opening):
        def step():
            if opening:
                pl.semaphore_wait(barrier, len(peers))
            copy(c).start()

        return step

    for c in range(wides):
        items = n // per_wide
        for q in range(4):
            store = storing(s.a_send.at[c], wide, BF16) if q < 2 else storing(s.a_acc, wide, F32)
            unit = matmul_unit(c * items, q * items // 4, (q + 1) * items // 4, wide_copies, store)
            line.append((4 * c + q, 0, unit))
        line.append((4 * c + 1, 1, send_core(core_copy, c, c == 0)))
        for order, (delay, step) in enumerate(zip(WIDE_DELAYS, (reduce_core, reduce_x, reduce_z, gather_x, gather_core, finish))):
            line.append((4 * c + 3 + delay, 2 + order, functools.partial(step, c)))
    for c in range(narrows):
        items = n * BLOCK // slot_w
        for q in range(2):
            store = storing(s.e_send.at[c], BLOCK, BF16) if q < 1 else storing(s.e_acc, BLOCK, F32)
            unit = matmul_unit(wide_items + c * items, q * items // 2, (q + 1) * items // 2, narrow_copies, store)
            line.append((4 * wides + 2 * c + q, 0, unit))
        line.append((4 * wides + 2 * c, 1, send_core(d_core_copy, c, False)))
        for order, (delay, step) in enumerate(zip(NARROW_DELAYS, (d_reduce_core, d_reduce, d_gather_core, d_finish))):
            line.append((4 * wides + 2 * c + 1 + delay, 2 + order, functools.partial(step, c)))
    for time, order, step in sorted(line, key=lambda entry: entry[:2]):
        step()

    for c in range(wides):
        core_copy(c).wait_send()
        gk_copy(c, mk).wait_send()
        for j in range(1, xs):
            x_copy(c, j).wait_send()
            gx_copy(c, j, mx).wait_send()
        for j in range(1, zs):
            z_copy(c, j).wait_send()
            gz_copy(c, j, mz).wait_send()
    for c in range(narrows):
        d_core_copy(c).wait_send()
        dgk_copy(c, mk).wait_send()
        for j in range(1, half):
            d_copy(c, j).wait_send()
            dg_copy(c, j, chip).wait_send()
    if narrows:
        for j in range(1, half):
            sd_copy(j).wait_send()
    else:
        for j in range(1, zs):
            sz_copy(j).wait_send()
        for j in range(1, xs):
            sx_copy(j).wait_send()
    sk_copy().wait_send()


def shards(hidden, down_weight, residual):
    n = lax.axis_size("tp")
    zs, xs = factor(n)
    half = zs * xs
    rows, depth = hidden.shape
    width = down_weight.shape[1]
    cols = width // n
    wides, w, narrows = plan(cols, n)
    dma = pltpu.SemaphoreType.DMA
    vmem = pltpu.VMEM
    scales = (rows, width // BLOCK)
    scratch = {
        "h": vmem((rows, depth), BF16),
        "h_sem": dma,
        "wbuf": vmem((SLOTS, depth, 2 * BLOCK), BF16),
        "w_sem": dma((SLOTS, 2)),
        "a_send": vmem((wides, xs, zs, rows, w), BF16),
        "a_recv": vmem((wides, xs, zs, rows, w), BF16),
        "a_acc": vmem((xs, zs, rows, w), F32),
        "b_send": vmem((wides, xs - 1, zs, rows, w), BF16),
        "b_recv": vmem((wides, xs - 1, zs, rows, w), BF16),
        "b_acc": vmem((wides, zs, rows, w), F32),
        "c_send": vmem((wides, zs - 1, rows, w), BF16),
        "c_recv": vmem((wides, zs - 1, rows, w), BF16),
        "c_acc": vmem((wides, rows, w), F32),
        "g": vmem((wides, 2, xs, zs, rows, w), BF16),
        "sc_acc": vmem(scales, F32),
        "sk": vmem((2,) + scales, BF16),
        "ssk": dma,
        "rsk": dma,
    }
    for name, shape in (("a", ()), ("b", (xs - 1,)), ("c", (zs - 1,)), ("gz", (zs - 1,)), ("gx", (xs - 1,)), ("gk", ())):
        scratch["s" + name] = dma((wides,) + shape)
        scratch["r" + name] = dma((wides,) + shape)
    if narrows:
        scratch.update({
            "e_send": vmem((narrows, xs, zs, rows, BLOCK), BF16),
            "e_recv": vmem((narrows, xs, zs, rows, BLOCK), BF16),
            "e_acc": vmem((xs, zs, rows, BLOCK), F32),
            "d_send": vmem((narrows, half - 1, rows, BLOCK), BF16),
            "d_recv": vmem((narrows, half - 1, rows, BLOCK), BF16),
            "d_acc": vmem((narrows, rows, BLOCK), F32),
            "dg": vmem((narrows, 2, xs, zs, rows, BLOCK), BF16),
            "sd_buf": vmem((half,) + scales, BF16),
            "ssd": dma((half - 1,)),
            "rsd": dma((half - 1,)),
        })
        for name, shape in (("e", ()), ("d", (half - 1,)), ("dg", (half - 1,)), ("dk", ())):
            scratch["s" + name] = dma((narrows,) + shape)
            scratch["r" + name] = dma((narrows,) + shape)
    else:
        scratch.update({
            "sz": vmem((zs,) + scales, BF16),
            "sx": vmem((xs,) + scales, BF16),
            "ssz": dma((zs - 1,)),
            "rsz": dma((zs - 1,)),
            "ssx": dma((xs - 1,)),
            "rsx": dma((xs - 1,)),
        })
    hbm = pl.BlockSpec(memory_space=pl.ANY)
    whole = pl.BlockSpec(memory_space=pltpu.VMEM)
    return pl.pallas_call(
        functools.partial(kernel, n, tuple(scratch)),
        out_shape=(
            jax.ShapeDtypeStruct((rows, width), BF16),
            jax.ShapeDtypeStruct(scales, BF16),
        ),
        in_specs=[hbm, hbm, whole],
        out_specs=(whole, whole),
        scratch_shapes=list(scratch.values()),
        compiler_params=pltpu.CompilerParams(collective_id=0, has_side_effects=True, vmem_limit_bytes=48 * 2**20),
        cost_estimate=pl.CostEstimate(
            flops=2 * rows * depth * width, bytes_accessed=2 * depth * width, transcendentals=0
        ),
    )(hidden, down_weight, residual)


def solution(mesh):
    in_specs = (P("groups", "tp"), P("tp", None), P("groups", "tp"))
    out_specs = (P("groups", None), P("groups", None))
    return jax.shard_map(shards, mesh=mesh, in_specs=in_specs, out_specs=out_specs, check_vma=False)
```
